512 devices in a mesh: dp: 64 (over z, y), mp: 8 (over x, core).
Axes of the slice: x: 4, y: 8, z: 8, core: 2. Of those that a mesh axis runs over, the one named last changes fastest.
Arguments:
- hidden_states: bfloat16 [65536, 8192], P('dp', 'mp'), may hold values from -6 to 6
- key_grad: bfloat16 [65536, 1024], P('dp'), may hold values from -0.23925781 to 0.23925781
- error_buffer: bfloat16 [64, 8192, 1024], P('dp', 'mp'), may hold values from -6 to 6
- q_init: float32 [1024, 32], replicated, may hold values from -6 to 6
Outputs:
- q_factor: float32 [1024, 32], P('mp')
The draws below stay inside these ranges and needn't reach their ends.
All inputs are finite; a program needn't handle non-finite values.
Results may differ from the reference program's by a relative error of at most 0.0003.
Values sent between devices are 32-bit elements; how exact they have to be, the bound alone decides.
No kernel may reach another device: no remote copies, remote signals or barrier semaphores. Data moves between devices by JAX's collectives and lax.ppermute only.
A program may use at most 64 MiB of HBM per device.

```python
import jax
import jax.numpy as jnp
from jax import lax

D = 8192
KV = 1024
RANK = 32
TOK_DEV = 1024
TOKENS = 65536
N_DP = 64


def shard_levels(key, dims, split, least, high):
    level = 1.0
    for axis_at, shards_of in split:
        steps = jax.random.uniform(jax.random.fold_in(jax.random.fold_in(key, 6), axis_at), (shards_of,), jnp.float32, least / len(split), high / len(split))
        level = level * jnp.repeat(jnp.exp(steps), dims[axis_at] // shards_of).reshape((-1,) + (1,) * (len(dims) - 1 - axis_at))
    return level


def bell_draw(key, dims, scale, reach, shards=(), kind=jnp.bfloat16):
    loudness = shard_levels(key, dims, shards, -0.22, 0.18) if shards else 1.0
    entries = jax.random.normal(key, dims, jnp.float32) * scale * loudness
    return jnp.minimum(jnp.maximum(entries, -reach), reach).astype(kind)


def setup_inputs(seed: int = 0) -> dict:
    seeds = jax.random.split(jax.random.key(seed), 5)
    hidden_states = bell_draw(seeds[0], (TOKENS, D), 1.0, 6.0, ((0, 64), (1, 8)))
    key_grad = bell_draw(seeds[1], (TOKENS, KV), 0.04, 0.23925781, ((0, 64),))
    error_buffer = bell_draw(seeds[2], (N_DP, D, KV), 1.0, 6.0, ((0, 64), (1, 8)))
    q_init = bell_draw(seeds[3], (KV, RANK), 1.0, 6.0, (), jnp.float32)
    return dict(hidden_states=hidden_states, key_grad=key_grad, error_buffer=error_buffer, q_init=q_init)


def reference(hidden_states, key_grad, error_buffer, q_init):
    inputs = hidden_states.reshape(N_DP, TOK_DEV, D)
    grads = key_grad.reshape(N_DP, TOK_DEV, KV)

    def accumulate(total, item):
        states, outgrad, residual = item
        gradient = jnp.dot(states.T.astype(jnp.float32), outgrad.astype(jnp.float32), preferred_element_type=jnp.float32)
        return (total + gradient + residual.astype(jnp.float32), None)
    start = jnp.zeros((D, KV), jnp.float32)
    summed, unused = lax.scan(accumulate, start, (inputs, grads, error_buffer))
    p_factor = jnp.dot(summed, q_init, precision=lax.Precision.HIGHEST) / N_DP
    gram = jnp.dot(p_factor.T, p_factor, precision=lax.Precision.HIGHEST)
    lower = jnp.linalg.cholesky(gram)
    basis = jax.scipy.linalg.solve_triangular(lower, p_factor.T, lower=True).T
    return jnp.dot(summed.T, basis, precision=lax.Precision.HIGHEST) / N_DP
```

```python
import jax
import jax.numpy as jnp
from jax import lax
from jax.sharding import Mesh, PartitionSpec as P

DP = ("zh", "zl", "yh", "yl")
MP = ("x", "core")
NEAR = ("zl", "yl", "x", "core")


def pieces(value):
    high = lax.reduce_precision(value, 8, 7)
    return jnp.concatenate([high, value - high], 0).astype(jnp.bfloat16)


def thin(left, right, contract):
    rank = left.shape[0]
    out = lax.dot_general(pieces(left), right, (((1,), (contract,)), ((), ())), preferred_element_type=jnp.float32)
    return out[:rank] + out[rank:]


def left_partial(hidden, key_grad, error, q_init):
    q_t = q_init.T
    u_t = thin(q_t, key_grad, 1)
    p_t = thin(u_t, hidden, 0) + thin(q_t, error, 1)
    return p_t.reshape(8, 4, 8, 128).transpose(2, 0, 1, 3).reshape(64, 4, 128)


def right_partial(hidden, key_grad, error, p_blocks):
    p_t = p_blocks.reshape(8, 8, 4, 128).transpose(1, 2, 0, 3).reshape(32, 1024)
    v_t = thin(p_t, hidden, 1)
    q_t = thin(v_t, key_grad, 0) + thin(p_t, error, 0)
    gram = jnp.dot(p_t, p_t.T, precision=lax.Precision.HIGHEST)
    blocks = q_t.reshape(4, 8, 8, 128).transpose(0, 2, 1, 3).reshape(32, 8, 128)
    packed = gram.reshape(4, 8, 32).transpose(1, 0, 2).reshape(1, 8, 128)
    return jnp.concatenate([blocks, jnp.broadcast_to(packed, (32, 8, 128))], 1)


def finish(blocks, packed):
    gram = packed.reshape(8, 4, 32).transpose(1, 0, 2).reshape(32, 32)
    q_t = blocks.reshape(4, 2, 4, 2, 8, 128).sum((0, 2)).reshape(32, 128)
    lower = jnp.linalg.cholesky(gram)
    return jax.scipy.linalg.solve_triangular(lower, q_t, lower=True).T


def shards(hidden, key_grad, error, q_init):
    part = left_partial(hidden, key_grad, error[0], q_init)
    part = lax.all_to_all(part, DP, 0, 0, tiled=True)
    own = part.sum(0) / 64
    p_blocks = lax.all_to_all(jnp.broadcast_to(own, (64, 4, 128)), DP, 0, 0, tiled=True)
    part = right_partial(hidden, key_grad, error[0], p_blocks)
    part = lax.all_to_all(part, NEAR, 0, 0, tiled=True)
    near = part.sum(0)
    packed = near[8:] * 0.25
    blocks = lax.all_to_all(jnp.broadcast_to(near[:8] / 64, (64, 8, 128)), DP, 0, 0, tiled=True)
    return finish(blocks, packed)


def solution(mesh):
    fine = Mesh(mesh.devices.reshape(4, 2, 4, 2, 4, 2), DP + MP)
    in_specs = (P(DP, MP), P(DP, None), P(DP, MP, None), P())
    return jax.shard_map(shards, mesh=fine, in_specs=in_specs, out_specs=P(MP, None), check_vma=False)
```

```python
import jax
import jax.experimental.pallas as pl
import jax.experimental.pallas.tpu as pltpu
import jax.numpy as jnp
from jax import lax
from jax.sharding import Mesh, PartitionSpec as P

DP = ("z2", "z1", "z0", "y2", "y1", "y0")
MP = ("x", "core")
LEFT_NEAR = ("z1", "z0", "y2", "y1", "y0")
RIGHT_NEAR = ("z0", "y0", "x", "core")

F32, BF16 = jnp.float32, jnp.bfloat16
RANK, WIDTH, HALF = 32, 1024, 512
NN = (((1,), (0,)), ((), ()))
NT = (((1,), (1,)), ((), ()))
VMEM = pl.BlockSpec(memory_space=pltpu.VMEM)
HBM = pl.BlockSpec(memory_space=pltpu.HBM)
PARAMS = pltpu.CompilerParams(vmem_limit_bytes=24 << 20)


def in_vmem(*arrays):
    return [pltpu.with_memory_space_constraint(a, pltpu.VMEM) for a in arrays]


def in_hbm(*arrays):
    return [pltpu.with_memory_space_constraint(a, pltpu.HBM) for a in arrays]


def dot(a, b, dims):
    return lax.dot_general(a, b, dims, preferred_element_type=F32)


def pieces(value):
    high = value.astype(BF16)
    return jnp.concatenate([high, (value - high.astype(F32)).astype(BF16)], 0)


def fold(product):
    return product[:RANK] + product[RANK:]


def left_kernel(q_hbm, key_hbm, error_hbm, hidden_hbm, out, key, error, hidden, q, acc, sems):
    first = pltpu.make_async_copy(q_hbm, q, sems.at[0])
    first.start()
    copies = []
    for source, target in ((key_hbm, key), (error_hbm, error), (hidden_hbm, hidden)):
        for at in range(0, WIDTH, HALF):
            rows = pl.ds(at, HALF)
            copies.append(pltpu.make_async_copy(source.at[rows, :], target.at[rows, :], sems.at[1 + len(copies)]))
            copies[-1].start()
    first.wait()
    q2 = pieces(q[...])
    inner = []
    for i in range(2):
        copies[i].wait()
        inner.append(pieces(fold(dot(q2, key[i * HALF:(i + 1) * HALF, :], NT))))
    for i in range(2):
        copies[2 + i].wait()
        acc[:, i * HALF:(i + 1) * HALF] = fold(dot(q2, error[i * HALF:(i + 1) * HALF, :], NT))
    copies[4].wait()
    total = dot(inner[0], hidden[:HALF, :], NN)
    copies[5].wait()
    total = fold(total + dot(inner[1], hidden[HALF:, :], NN)) + acc[...]
    for k in range(32):
        out[k] = total[8 * (k % 4):8 * (k % 4) + 8, 128 * (k // 4):128 * (k // 4) + 128]


def left_partial(q_t, key, error, hidden):
    big = pltpu.VMEM((WIDTH, WIDTH), BF16)
    thin = pltpu.VMEM((RANK, WIDTH), F32)
    return pl.pallas_call(
        left_kernel,
        out_shape=(pltpu.VMEM((32, 8, 128), F32), big, big, big),
        in_specs=[HBM] * 4,
        out_specs=(VMEM,) * 4,
        scratch_shapes=[thin, thin, pltpu.SemaphoreType.DMA((7,))],
        compiler_params=PARAMS,
        name="left_partial",
    )(*in_hbm(q_t, key, error, hidden))


def left_sum_kernel(parts, out):
    total = jnp.sum(parts[...], 0)
    for k in range(64):
        out[k] = total


def left_sum(parts):
    return pl.pallas_call(
        left_sum_kernel,
        out_shape=pltpu.VMEM((64, 8, 128), F32),
        in_specs=[VMEM],
        out_specs=VMEM,
        compiler_params=PARAMS,
        name="left_sum",
    )(*in_vmem(parts))


def right_kernel(tiles, key, error, hidden, out):
    columns = [
        jnp.concatenate([tiles[4 * b + a] + tiles[32 + 4 * b + a] for a in range(4)], 0) for b in range(8)
    ]
    p2 = pieces(jnp.concatenate(columns, 1) * (1 / 64))
    inner = pieces(fold(dot(p2, hidden[...], NT)))
    total = fold(dot(p2, error[...], NN) + dot(inner, key[...], NN)) * (1 / 64)
    gram = fold(dot(p2, p2, NT))
    gram = (gram[:, :RANK] + gram[:, RANK:]) * 0.25
    packed = jnp.concatenate([gram[8 * s:8 * s + 8] for s in range(4)], 1)
    for k in range(32):
        s, m = k // 8, k % 8
        out[k, :8] = total[8 * s:8 * s + 8, 128 * m:128 * m + 128]
        out[k, 8:] = packed


def right_partial(tiles, key, error, hidden):
    return pl.pallas_call(
        right_kernel,
        out_shape=pltpu.VMEM((32, 16, 128), F32),
        in_specs=[VMEM] * 4,
        out_specs=VMEM,
        compiler_params=PARAMS,
        name="right_partial",
    )(*in_vmem(tiles, key, error, hidden))


def right_sum_kernel(parts, out, gram):
    total = jnp.sum(parts[...], 0)
    for k in range(64):
        out[k] = total[:8]
    for s in range(4):
        gram[8 * s:8 * s + 8, :] = total[8:, RANK * s:RANK * s + RANK]


def right_sum(parts):
    return pl.pallas_call(
        right_sum_kernel,
        out_shape=(pltpu.VMEM((64, 8, 128), F32), pltpu.VMEM((RANK, RANK), F32)),
        in_specs=[VMEM],
        out_specs=(VMEM, VMEM),
        compiler_params=PARAMS,
        name="right_sum",
    )(*in_vmem(parts))


def finish_kernel(tiles, inverse, out):
    rows = []
    for s in range(4):
        total = tiles[s // 2 * 8 + s % 2]
        for r in range(1, 16):
            total = total + tiles[r // 4 * 16 + s // 2 * 8 + r % 4 * 2 + s % 2]
        rows.append(total)
    out[...] = jnp.dot(inverse[...], jnp.concatenate(rows, 0), precision=lax.Precision.HIGHEST, preferred_element_type=F32)


def finish(tiles, inverse):
    return pl.pallas_call(
        finish_kernel,
        out_shape=jax.ShapeDtypeStruct((RANK, 128), F32),
        in_specs=[VMEM, VMEM],
        out_specs=VMEM,
        compiler_params=PARAMS,
        name="finish",
    )(*in_vmem(tiles, inverse))


def shards(hidden, key, error, q_init):
    error = error[0]
    part, key, error, hidden = left_partial(q_init.T, key, error, hidden)
    part = lax.all_to_all(part, LEFT_NEAR, 0, 0, tiled=True)
    tiles = lax.all_to_all(left_sum(part), DP, 0, 0, tiled=True)
    part = lax.all_to_all(right_partial(tiles, key, error, hidden), RIGHT_NEAR, 0, 0, tiled=True)
    tiles, gram = right_sum(part)
    tiles = lax.all_to_all(tiles, DP, 0, 0, tiled=True)
    lower = jnp.linalg.cholesky(gram)
    inverse = jax.scipy.linalg.solve_triangular(lower, jnp.eye(RANK, dtype=F32), lower=True)
    return finish(tiles, inverse).T


def solution(mesh):
    fine = Mesh(mesh.devices.reshape(2, 2, 2, 2, 2, 2, 4, 2), DP + MP)
    in_specs = (P(DP, MP), P(DP, None), P(DP, MP, None), P())
    return jax.shard_map(shards, mesh=fine, in_specs=in_specs, out_specs=P(MP, None), check_vma=False)
```

```python
import jax
import jax.experimental.pallas as pl
import jax.experimental.pallas.tpu as pltpu
import jax.numpy as jnp
from jax import lax
from jax.sharding import Mesh, PartitionSpec as P

DP = ("z2", "z1", "z0", "y2", "y1", "y0")
MP = ("x", "core")
LEFT_NEAR = ("z1", "z0", "y2", "y1", "y0")
RIGHT_NEAR = ("z0", "y0", "x", "core")

F32, BF16 = jnp.float32, jnp.bfloat16
RANK, WIDTH, HALF = 32, 1024, 512
NN = (((1,), (0,)), ((), ()))
NT = (((1,), (1,)), ((), ()))
VMEM = pl.BlockSpec(memory_space=pltpu.VMEM)
HBM = pl.BlockSpec(memory_space=pltpu.HBM)
PARAMS = pltpu.CompilerParams(vmem_limit_bytes=24 << 20)


def in_vmem(*arrays):
    return [pltpu.with_memory_space_constraint(a, pltpu.VMEM) for a in arrays]


def in_hbm(*arrays):
    return [pltpu.with_memory_space_constraint(a, pltpu.HBM) for a in arrays]


def dot(a, b, dims):
    return lax.dot_general(a, b, dims, preferred_element_type=F32)


def pieces(value):
    parts = []
    for _ in range(3):
        parts.append(value.astype(BF16))
        value = value - parts[-1].astype(F32)
    return jnp.concatenate(parts, 0)


def fold(product):
    return product[:RANK] + product[RANK:2 * RANK] + product[2 * RANK:]


def left_kernel(q_hbm, key_hbm, error_hbm, hidden_hbm, out, key, error, hidden, q, acc, sems):
    first = pltpu.make_async_copy(q_hbm, q, sems.at[0])
    first.start()
    copies = []
    for source, target in ((key_hbm, key), (error_hbm, error), (hidden_hbm, hidden)):
        for at in range(0, WIDTH, HALF):
            rows = pl.ds(at, HALF)
            copies.append(pltpu.make_async_copy(source.at[rows, :], target.at[rows, :], sems.at[1 + len(copies)]))
            copies[-1].start()
    first.wait()
    q2 = pieces(q[...])
    inner = []
    for i in range(2):
        copies[i].wait()
        inner.append(pieces(fold(dot(q2, key[i * HALF:(i + 1) * HALF, :], NT))))
    for i in range(2):
        copies[2 + i].wait()
        acc[:, i * HALF:(i + 1) * HALF] = fold(dot(q2, error[i * HALF:(i + 1) * HALF, :], NT))
    copies[4].wait()
    total = dot(inner[0], hidden[:HALF, :], NN)
    copies[5].wait()
    total = fold(total + dot(inner[1], hidden[HALF:, :], NN)) + acc[...]
    for k in range(32):
        out[k] = total[8 * (k % 4):8 * (k % 4) + 8, 128 * (k // 4):128 * (k // 4) + 128]


def left_partial(q_t, key, error, hidden):
    big = pltpu.VMEM((WIDTH, WIDTH), BF16)
    thin = pltpu.VMEM((RANK, WIDTH), F32)
    return pl.pallas_call(
        left_kernel,
        out_shape=(pltpu.VMEM((32, 8, 128), F32), big, big, big),
        in_specs=[HBM] * 4,
        out_specs=(VMEM,) * 4,
        scratch_shapes=[thin, thin, pltpu.SemaphoreType.DMA((7,))],
        compiler_params=PARAMS,
        name="left_partial",
    )(*in_hbm(q_t, key, error, hidden))


def left_sum_kernel(parts, out):
    total = jnp.sum(parts[...], 0)
    for k in range(64):
        out[k] = total


def left_sum(parts):
    return pl.pallas_call(
        left_sum_kernel,
        out_shape=pltpu.VMEM((64, 8, 128), F32),
        in_specs=[VMEM],
        out_specs=VMEM,
        compiler_params=PARAMS,
        name="left_sum",
    )(*in_vmem(parts))


def right_kernel(tiles, key, error, hidden, out):
    columns = [
        jnp.concatenate([tiles[4 * b + a] + tiles[32 + 4 * b + a] for a in range(4)], 0) for b in range(8)
    ]
    p2 = pieces(jnp.concatenate(columns, 1) * (1 / 64))
    inner = pieces(fold(dot(p2, hidden[...], NT)))
    total = fold(dot(p2, error[...], NN) + dot(inner, key[...], NN)) * (1 / 64)
    gram = fold(dot(p2, p2, NT))
    gram = (gram[:, :RANK] + gram[:, RANK:2 * RANK] + gram[:, 2 * RANK:]) * 0.25
    packed = jnp.concatenate([gram[8 * s:8 * s + 8] for s in range(4)], 1)
    for k in range(32):
        s, m = k // 8, k % 8
        out[k, :8] = total[8 * s:8 * s + 8, 128 * m:128 * m + 128]
        out[k, 8:] = packed


def right_partial(tiles, key, error, hidden):
    return pl.pallas_call(
        right_kernel,
        out_shape=pltpu.VMEM((32, 16, 128), F32),
        in_specs=[VMEM] * 4,
        out_specs=VMEM,
        compiler_params=PARAMS,
        name="right_partial",
    )(*in_vmem(tiles, key, error, hidden))


def right_sum_kernel(parts, out, gram):
    total = jnp.sum(parts[...], 0)
    for k in range(64):
        out[k] = total[:8]
    for s in range(4):
        gram[8 * s:8 * s + 8, :] = pltpu.roll(total[8:], 128 - RANK * s, 1) if s else total[8:]


def right_sum(parts):
    return pl.pallas_call(
        right_sum_kernel,
        out_shape=(pltpu.VMEM((64, 8, 128), F32), pltpu.VMEM((RANK, 128), F32)),
        in_specs=[VMEM],
        out_specs=(VMEM, VMEM),
        compiler_params=PARAMS,
        name="right_sum",
    )(*in_vmem(parts))


def along_lanes(tile, j):
    return jnp.broadcast_to(tile[:, j:j + 1], (8, 128))


def along_rows(tile, j):
    return jnp.broadcast_to(tile[j:j + 1, :], (8, 128))


def finish_kernel(tiles, gram, out):
    rows = []
    for s in range(4):
        total = tiles[s // 2 * 8 + s % 2]
        for r in range(1, 16):
            total = total + tiles[r // 4 * 16 + s // 2 * 8 + r % 4 * 2 + s % 2]
        rows.append(total)
    rest = [gram[8 * s:8 * s + 8, :] for s in range(4)]
    row = lax.broadcasted_iota(jnp.int32, (8, 128), 0)
    for b in range(4):
        column = {s: [along_lanes(rest[s], 8 * b + q) for q in range(8)] for s in range(b, 4)}
        block = [[along_rows(column[b][q], p) for q in range(p + 1)] for p in range(8)]
        pivot_rest = [along_rows(rest[b], p) for p in range(8)]
        pivot_rows = [along_rows(rows[b], p) for p in range(8)]
        inverse = []
        for q in range(8):
            inverse.append(1.0 / block[q][q])
            for p in range(q + 1, 8):
                factor = block[p][q] * inverse[q]
                pivot_rest[p] = pivot_rest[p] - factor * pivot_rest[q]
                pivot_rows[p] = pivot_rows[p] - factor * pivot_rows[q]
                for t in range(q + 1, p + 1):
                    block[p][t] = block[p][t] - factor * block[t][q]
        for s in range(b, 4):
            for q in range(8):
                factor = column[s][q] * inverse[q]
                if s == b:
                    factor = jnp.where(row > q, factor, 0.0)
                for t in range(q + 1, 8):
                    column[s][t] = column[s][t] - factor * block[t][q]
                rest[s] = rest[s] - factor * pivot_rest[q]
                rows[s] = rows[s] - factor * pivot_rows[q]
        scale = lax.rsqrt(block[0][0])
        for q in range(1, 8):
            scale = jnp.where(row == q, lax.rsqrt(block[q][q]), scale)
        out[8 * b:8 * b + 8, :] = rows[b] * scale


def finish(tiles, gram):
    return pl.pallas_call(
        finish_kernel,
        out_shape=jax.ShapeDtypeStruct((RANK, 128), F32),
        in_specs=[VMEM, VMEM],
        out_specs=VMEM,
        compiler_params=PARAMS,
        name="finish",
    )(*in_vmem(tiles, gram))


def shards(hidden, key, error, q_init):
    error = error[0]
    part, key, error, hidden = left_partial(q_init.T, key, error, hidden)
    part = lax.all_to_all(part, LEFT_NEAR, 0, 0, tiled=True)
    tiles = lax.all_to_all(left_sum(part), DP, 0, 0, tiled=True)
    part = lax.all_to_all(right_partial(tiles, key, error, hidden), RIGHT_NEAR, 0, 0, tiled=True)
    tiles, gram = right_sum(part)
    return finish(lax.all_to_all(tiles, DP, 0, 0, tiled=True), gram).T


def solution(mesh):
    fine = Mesh(mesh.devices.reshape(2, 2, 2, 2, 2, 2, 4, 2), DP + MP)
    in_specs = (P(DP, MP), P(DP, None), P(DP, MP, None), P())
    return jax.shard_map(shards, mesh=fine, in_specs=in_specs, out_specs=P(MP, None), check_vma=False)
```

```python
import jax
import jax.experimental.pallas as pl
import jax.experimental.pallas.tpu as pltpu
import jax.numpy as jnp
from jax import lax
from jax.sharding import Mesh, PartitionSpec as P

DP = ("z2", "z1", "z0", "y2", "y1", "y0")
MP = ("x", "core")
RIGHT_NEAR = ("z0", "y0", "x", "core")

F32, BF16 = jnp.float32, jnp.bfloat16
RANK, WIDTH, HALF = 32, 1024, 512
NN = (((1,), (0,)), ((), ()))
NT = (((1,), (1,)), ((), ()))
VMEM = pl.BlockSpec(memory_space=pltpu.VMEM)
HBM = pl.BlockSpec(memory_space=pltpu.HBM)
PARAMS = pltpu.CompilerParams(vmem_limit_bytes=24 << 20)


def in_vmem(*arrays):
    return [pltpu.with_memory_space_constraint(a, pltpu.VMEM) for a in arrays]


def in_hbm(*arrays):
    return [pltpu.with_memory_space_constraint(a, pltpu.HBM) for a in arrays]


def dot(a, b, dims):
    return lax.dot_general(a, b, dims, preferred_element_type=F32)


def pieces(value):
    parts = []
    for _ in range(3):
        parts.append(value.astype(BF16))
        value = value - parts[-1].astype(F32)
    return jnp.concatenate(parts, 0)


def fold(product):
    return product[:RANK] + product[RANK:2 * RANK] + product[2 * RANK:]


def left_kernel(q_hbm, key_hbm, error_hbm, hidden_hbm, out, key, error, hidden, q, acc, sems):
    first = pltpu.make_async_copy(q_hbm, q, sems.at[0])
    first.start()
    copies = []
    for source, target in ((key_hbm, key), (error_hbm, error), (hidden_hbm, hidden)):
        for at in range(0, WIDTH, HALF):
            rows = pl.ds(at, HALF)
            copies.append(pltpu.make_async_copy(source.at[rows, :], target.at[rows, :], sems.at[1 + len(copies)]))
            copies[-1].start()
    first.wait()
    q2 = pieces(q[...])
    inner = []
    for i in range(2):
        copies[i].wait()
        inner.append(pieces(fold(dot(q2, key[i * HALF:(i + 1) * HALF, :], NT))))
    for i in range(2):
        copies[2 + i].wait()
        acc[:, i * HALF:(i + 1) * HALF] = fold(dot(q2, error[i * HALF:(i + 1) * HALF, :], NT))
    copies[4].wait()
    total = dot(inner[0], hidden[:HALF, :], NN)
    copies[5].wait()
    total = fold(total + dot(inner[1], hidden[HALF:, :], NN)) + acc[...]
    for k in range(32):
        out[k] = total[8 * (k % 4):8 * (k % 4) + 8, 128 * (k // 4):128 * (k // 4) + 128]


def left_partial(q_t, key, error, hidden):
    big = pltpu.VMEM((WIDTH, WIDTH), BF16)
    thin = pltpu.VMEM((RANK, WIDTH), F32)
    return pl.pallas_call(
        left_kernel,
        out_shape=(pltpu.VMEM((32, 8, 128), F32), big, big, big),
        in_specs=[HBM] * 4,
        out_specs=(VMEM,) * 4,
        scratch_shapes=[thin, thin, pltpu.SemaphoreType.DMA((7,))],
        compiler_params=PARAMS,
        name="left_partial",
    )(*in_hbm(q_t, key, error, hidden))


def left_sum_kernel(parts, out):
    total = jnp.sum(parts[...], 0)
    total = total + pltpu.roll(total, 4, 0)
    for k in range(32):
        out[k] = total


def left_sum(parts):
    return pl.pallas_call(
        left_sum_kernel,
        out_shape=pltpu.VMEM((32, 8, 128), F32),
        in_specs=[VMEM],
        out_specs=VMEM,
        compiler_params=PARAMS,
        name="left_sum",
    )(*in_vmem(parts))


def right_kernel(tiles, key, error, hidden, out):
    columns = [
        jnp.concatenate([tiles[4 * b + a] for a in range(4)], 0) for b in range(8)
    ]
    p2 = pieces(jnp.concatenate(columns, 1) * (1 / 64))
    inner = pieces(fold(dot(p2, hidden[...], NT)))
    total = fold(dot(p2, error[...], NN) + dot(inner, key[...], NN)) * (1 / 64)
    gram = fold(dot(p2, p2, NT))
    gram = (gram[:, :RANK] + gram[:, RANK:2 * RANK] + gram[:, 2 * RANK:]) * 0.25
    packed = jnp.concatenate([gram[8 * s:8 * s + 8] for s in range(4)], 1)
    for k in range(32):
        s, m = k // 8, k % 8
        out[k, :8] = total[8 * s:8 * s + 8, 128 * m:128 * m + 128]
        out[k, 8:] = packed


def right_partial(tiles, key, error, hidden):
    return pl.pallas_call(
        right_kernel,
        out_shape=pltpu.VMEM((32, 16, 128), F32),
        in_specs=[VMEM] * 4,
        out_specs=VMEM,
        compiler_params=PARAMS,
        name="right_partial",
    )(*in_vmem(tiles, key, error, hidden))


def right_sum_kernel(parts, out, gram):
    total = jnp.sum(parts[...], 0)
    for k in range(64):
        out[k] = total[:8]
    for s in range(4):
        gram[8 * s:8 * s + 8, :] = pltpu.roll(total[8:], 128 - RANK * s, 1) if s else total[8:]


def right_sum(parts):
    return pl.pallas_call(
        right_sum_kernel,
        out_shape=(pltpu.VMEM((64, 8, 128), F32), pltpu.VMEM((RANK, 128), F32)),
        in_specs=[VMEM],
        out_specs=(VMEM, VMEM),
        compiler_params=PARAMS,
        name="right_sum",
    )(*in_vmem(parts))


def along_lanes(tile, j):
    return jnp.broadcast_to(tile[:, j:j + 1], (8, 128))


def along_rows(tile, j):
    return jnp.broadcast_to(tile[j:j + 1, :], (8, 128))


def finish_kernel(tiles, gram, out):
    rows = []
    for s in range(4):
        total = tiles[s // 2 * 8 + s % 2]
        for r in range(1, 16):
            total = total + tiles[r // 4 * 16 + s // 2 * 8 + r % 4 * 2 + s % 2]
        rows.append(total)
    rest = [gram[8 * s:8 * s + 8, :] for s in range(4)]
    row = lax.broadcasted_iota(jnp.int32, (8, 128), 0)
    for b in range(4):
        column = {s: [along_lanes(rest[s], 8 * b + q) for q in range(8)] for s in range(b, 4)}
        block = [[along_rows(column[b][q], p) for q in range(p + 1)] for p in range(8)]
        pivot_rest = [along_rows(rest[b], p) for p in range(8)]
        pivot_rows = [along_rows(rows[b], p) for p in range(8)]
        inverse = []
        for q in range(8):
            inverse.append(1.0 / block[q][q])
            for p in range(q + 1, 8):
                factor = block[p][q] * inverse[q]
                pivot_rest[p] = pivot_rest[p] - factor * pivot_rest[q]
                pivot_rows[p] = pivot_rows[p] - factor * pivot_rows[q]
                for t in range(q + 1, p + 1):
                    block[p][t] = block[p][t] - factor * block[t][q]
        for s in range(b, 4):
            for q in range(8):
                factor = column[s][q] * inverse[q]
                if s == b:
                    factor = jnp.where(row > q, factor, 0.0)
                for t in range(q + 1, 8):
                    column[s][t] = column[s][t] - factor * block[t][q]
                rest[s] = rest[s] - factor * pivot_rest[q]
                rows[s] = rows[s] - factor * pivot_rows[q]
        scale = lax.rsqrt(block[0][0])
        for q in range(1, 8):
            scale = jnp.where(row == q, lax.rsqrt(block[q][q]), scale)
        out[8 * b:8 * b + 8, :] = rows[b] * scale


def finish(tiles, gram):
    return pl.pallas_call(
        finish_kernel,
        out_shape=jax.ShapeDtypeStruct((RANK, 128), F32),
        in_specs=[VMEM, VMEM],
        out_specs=VMEM,
        compiler_params=PARAMS,
        name="finish",
    )(*in_vmem(tiles, gram))


def halves_over_dp(tiles):
    return lax.all_to_all(tiles.reshape(64, 4, 128), DP, 0, 0, tiled=True).reshape(32, 8, 128)


def shards(hidden, key, error, q_init):
    error = error[0]
    part, key, error, hidden = left_partial(q_init.T, key, error, hidden)
    tiles = halves_over_dp(left_sum(halves_over_dp(part)))
    part = lax.all_to_all(right_partial(tiles, key, error, hidden), RIGHT_NEAR, 0, 0, tiled=True)
    tiles, gram = right_sum(part)
    return finish(lax.all_to_all(tiles, DP, 0, 0, tiled=True), gram).T


def solution(mesh):
    fine = Mesh(mesh.devices.reshape(2, 2, 2, 2, 2, 2, 4, 2), DP + MP)
    in_specs = (P(DP, MP), P(DP, None), P(DP, MP, None), P())
    return jax.shard_map(shards, mesh=fine, in_specs=in_specs, out_specs=P(MP, None), check_vma=False)
```

```python
import jax
import jax.experimental.pallas as pl
import jax.experimental.pallas.tpu as pltpu
import jax.numpy as jnp
from jax import lax
from jax.sharding import Mesh, PartitionSpec as P

DP = ("z2", "z1", "z0", "y2", "y1", "y0")
MP = ("x", "core")
STEP_DP = ("y0", "z0", "y1", "z1", "y2", "z2")
NEAR = ("x", "core", "z0", "y0")

F32, BF16 = jnp.float32, jnp.bfloat16
RANK, WIDTH, HALF = 32, 1024, 512
ROWS = 10
NN = (((1,), (0,)), ((), ()))
NT = (((1,), (1,)), ((), ()))
VMEM = pl.BlockSpec(memory_space=pltpu.VMEM)
HBM = pl.BlockSpec(memory_space=pltpu.HBM)
PARAMS = pltpu.CompilerParams(vmem_limit_bytes=24 << 20)


def in_vmem(*arrays):
    return [pltpu.with_memory_space_constraint(a, pltpu.VMEM) for a in arrays]


def in_hbm(*arrays):
    return [pltpu.with_memory_space_constraint(a, pltpu.HBM) for a in arrays]


def dot(a, b, dims):
    return lax.dot_general(a, b, dims, preferred_element_type=F32)


def pieces(value):
    parts = []
    for _ in range(3):
        parts.append(value.astype(BF16))
        value = value - parts[-1].astype(F32)
    return jnp.concatenate(parts, 0)


def fold(product):
    return product[:RANK] + product[RANK:2 * RANK] + product[2 * RANK:]


def left_kernel(q_hbm, key_hbm, error_hbm, hidden_hbm, out, key, error, hidden, q, acc, sems):
    first = pltpu.make_async_copy(q_hbm, q, sems.at[0])
    first.start()
    copies = []
    for source, target in ((key_hbm, key), (error_hbm, error), (hidden_hbm, hidden)):
        for at in range(0, WIDTH, HALF):
            rows = pl.ds(at, HALF)
            copies.append(pltpu.make_async_copy(source.at[rows, :], target.at[rows, :], sems.at[1 + len(copies)]))
            copies[-1].start()
    first.wait()
    q2 = pieces(q[...])
    inner = []
    for i in range(2):
        copies[i].wait()
        inner.append(pieces(fold(dot(q2, key[i * HALF:(i + 1) * HALF, :], NT))))
    for i in range(2):
        copies[2 + i].wait()
        acc[:, i * HALF:(i + 1) * HALF] = fold(dot(q2, error[i * HALF:(i + 1) * HALF, :], NT))
    copies[4].wait()
    total = dot(inner[0], hidden[:HALF, :], NN)
    copies[5].wait()
    total = fold(total + dot(inner[1], hidden[HALF:, :], NN)) + acc[...]
    for k in range(32):
        out[k] = total[8 * (k % 4):8 * (k % 4) + 8, 128 * (k // 4):128 * (k // 4) + 128]


def left_partial(q_t, key, error, hidden):
    big = pltpu.VMEM((WIDTH, WIDTH), BF16)
    thin = pltpu.VMEM((RANK, WIDTH), F32)
    return pl.pallas_call(
        left_kernel,
        out_shape=(pltpu.VMEM((32, 8, 128), F32), big, big, big),
        in_specs=[HBM] * 4,
        out_specs=(VMEM,) * 4,
        scratch_shapes=[thin, thin, pltpu.SemaphoreType.DMA((7,))],
        compiler_params=PARAMS,
        name="left_partial",
    )(*in_hbm(q_t, key, error, hidden))


def left_sum_kernel(parts, out):
    total = jnp.sum(parts[...], 0)
    total = total + pltpu.roll(total, 4, 0)
    for k in range(32):
        out[k] = total


def left_sum(parts):
    return pl.pallas_call(
        left_sum_kernel,
        out_shape=pltpu.VMEM((32, 8, 128), F32),
        in_specs=[VMEM],
        out_specs=VMEM,
        compiler_params=PARAMS,
        name="left_sum",
    )(*in_vmem(parts))


def right_kernel(tiles, key, error, hidden, out, gram):
    columns = [
        jnp.concatenate([tiles[4 * b + a] for a in range(4)], 0) for b in range(8)
    ]
    p3 = pieces(jnp.concatenate(columns, 1) * (1 / 64))
    inner = pieces(fold(dot(p3, hidden[...], NT)))
    total = fold(dot(p3, error[...], NN) + dot(inner, key[...], NN)) * (1 / 64)
    square = fold(dot(p3, p3, NT))
    gram[...] = square[:, :RANK] + square[:, RANK:2 * RANK] + square[:, 2 * RANK:]
    quarter = 2 * lax.axis_index("z0") + lax.axis_index("y0")
    own = gram[pl.ds(pl.multiple_of(8 * quarter, 8), 8), :]
    packed = jnp.concatenate([own[2 * i:2 * i + 2] for i in range(4)], 1)
    for m in range(8):
        for s in range(4):
            at = ROWS * (4 * m + s)
            out[at:at + 8, :] = total[8 * s:8 * s + 8, 128 * m:128 * m + 128]
            out[at + 8:at + ROWS, :] = packed


def right_partial(tiles, key, error, hidden):
    return pl.pallas_call(
        right_kernel,
        out_shape=pltpu.VMEM((32 * ROWS, 128), F32),
        in_specs=[VMEM] * 4,
        out_specs=VMEM,
        scratch_shapes=[pltpu.VMEM((RANK, RANK), F32)],
        compiler_params=PARAMS,
        name="right_partial",
    )(*in_vmem(tiles, key, error, hidden))


def right_sum_kernel(parts, out, gram):
    total = parts[:8, :]
    for k in range(1, 32):
        total = total + parts[ROWS * k:ROWS * k + 8, :]
    for k in range(64):
        out[k] = total
    for s in range(4):
        packed = parts[ROWS * s + 8:ROWS * s + ROWS, :]
        for m in range(1, 8):
            at = ROWS * (4 * m + s)
            packed = packed + parts[at + 8:at + ROWS, :]
        for i in range(4):
            gram[8 * s + 2 * i:8 * s + 2 * i + 2, :RANK] = packed[:, RANK * i:RANK * i + RANK]


def right_sum(parts):
    return pl.pallas_call(
        right_sum_kernel,
        out_shape=(pltpu.VMEM((64, 8, 128), F32), pltpu.VMEM((RANK, 128), F32)),
        in_specs=[VMEM],
        out_specs=(VMEM, VMEM),
        compiler_params=PARAMS,
        name="right_sum",
    )(*in_vmem(parts))


def along_lanes(tile, j):
    return jnp.broadcast_to(tile[:, j:j + 1], (8, 128))


def along_rows(tile, j):
    return jnp.broadcast_to(tile[j:j + 1, :], (8, 128))


def finish_kernel(tiles, gram, out):
    rows = [jnp.sum(tiles[16 * s:16 * s + 16], 0) for s in (0, 2, 1, 3)]
    rest = [gram[8 * s:8 * s + 8, :] for s in range(4)]
    row = lax.broadcasted_iota(jnp.int32, (8, 128), 0)
    for b in range(4):
        column = {s: [along_lanes(rest[s], 8 * b + q) for q in range(8)] for s in range(b, 4)}
        block = [[along_rows(column[b][q], p) for q in range(p + 1)] for p in range(8)]
        pivot_rest = [along_rows(rest[b], p) for p in range(8)]
        pivot_rows = [along_rows(rows[b], p) for p in range(8)]
        inverse = []
        for q in range(8):
            inverse.append(1.0 / block[q][q])
            for p in range(q + 1, 8):
                factor = block[p][q] * inverse[q]
                pivot_rest[p] = pivot_rest[p] - factor * pivot_rest[q]
                pivot_rows[p] = pivot_rows[p] - factor * pivot_rows[q]
                for t in range(q + 1, p + 1):
                    block[p][t] = block[p][t] - factor * block[t][q]
        for s in range(b, 4):
            for q in range(8):
                factor = column[s][q] * inverse[q]
                if s == b:
                    factor = jnp.where(row > q, factor, 0.0)
                for t in range(q + 1, 8):
                    column[s][t] = column[s][t] - factor * block[t][q]
                rest[s] = rest[s] - factor * pivot_rest[q]
                rows[s] = rows[s] - factor * pivot_rows[q]
        scale = lax.rsqrt(block[0][0])
        for q in range(1, 8):
            scale = jnp.where(row == q, lax.rsqrt(block[q][q]), scale)
        out[8 * b:8 * b + 8, :] = rows[b] * scale


def finish(tiles, gram):
    return pl.pallas_call(
        finish_kernel,
        out_shape=jax.ShapeDtypeStruct((RANK, 128), F32),
        in_specs=[VMEM, VMEM],
        out_specs=VMEM,
        compiler_params=PARAMS,
        name="finish",
    )(*in_vmem(tiles, gram))


def halves_over_dp(tiles):
    return lax.all_to_all(tiles.reshape(64, 4, 128), STEP_DP, 0, 0, tiled=True).reshape(32, 8, 128)


def shards(hidden, key, error, q_init):
    error = error[0]
    part, key, error, hidden = left_partial(q_init.T, key, error, hidden)
    tiles = halves_over_dp(left_sum(halves_over_dp(part)))
    part = right_partial(tiles, key, error, hidden).reshape(-1, 2, 128)
    part = lax.all_to_all(part, NEAR, 0, 0, tiled=True).reshape(-1, 128)
    tiles, gram = right_sum(part)
    return finish(lax.all_to_all(tiles, STEP_DP, 0, 0, tiled=True), gram).T


def solution(mesh):
    fine = Mesh(mesh.devices.reshape(2, 2, 2, 2, 2, 2, 4, 2), DP + MP)
    in_specs = (P(DP, MP), P(DP, None), P(DP, MP, None), P())
    return jax.shard_map(shards, mesh=fine, in_specs=in_specs, out_specs=P(MP, None), check_vma=False)
```

```python
import jax
import jax.experimental.pallas as pl
import jax.experimental.pallas.tpu as pltpu
import jax.numpy as jnp
from jax import lax
from jax.sharding import Mesh, PartitionSpec as P

DP = ("z2", "z1", "z0", "y2", "y1", "y0")
MP = ("x", "core")
STEP_DP = ("y0", "z0", "y1", "z1", "y2", "z2")
NEAR = ("x", "core", "z0", "y0")

F32, BF16 = jnp.float32, jnp.bfloat16
RANK, WIDTH, HALF = 32, 1024, 512
ROWS = 10
NN = (((1,), (0,)), ((), ()))
NT = (((1,), (1,)), ((), ()))
VMEM = pl.BlockSpec(memory_space=pltpu.VMEM)
HBM = pl.BlockSpec(memory_space=pltpu.HBM)
PARAMS = pltpu.CompilerParams(vmem_limit_bytes=24 << 20)


def in_vmem(*arrays):
    return [pltpu.with_memory_space_constraint(a, pltpu.VMEM) for a in arrays]


def in_hbm(*arrays):
    return [pltpu.with_memory_space_constraint(a, pltpu.HBM) for a in arrays]


def dot(a, b, dims):
    return lax.dot_general(a, b, dims, preferred_element_type=F32)


def pieces(value):
    parts = []
    for _ in range(3):
        parts.append(value.astype(BF16))
        value = value - parts[-1].astype(F32)
    return jnp.concatenate(parts, 0)


def fold(product):
    return product[:RANK] + product[RANK:2 * RANK] + product[2 * RANK:]


def left_kernel(q_hbm, key_hbm, error_hbm, hidden_hbm, out, key, error, hidden, q, acc, sems):
    first = pltpu.make_async_copy(q_hbm, q, sems.at[0])
    first.start()
    copies = []
    for source, target in ((key_hbm, key), (error_hbm, error), (hidden_hbm, hidden)):
        for at in range(0, WIDTH, HALF):
            rows = pl.ds(at, HALF)
            copies.append(pltpu.make_async_copy(source.at[rows, :], target.at[rows, :], sems.at[1 + len(copies)]))
            copies[-1].start()
    first.wait()
    q2 = pieces(q[...])
    inner = []
    for i in range(2):
        copies[i].wait()
        inner.append(pieces(fold(dot(q2, key[i * HALF:(i + 1) * HALF, :], NT))))
    for i in range(2):
        copies[2 + i].wait()
        acc[:, i * HALF:(i + 1) * HALF] = fold(dot(q2, error[i * HALF:(i + 1) * HALF, :], NT))
    for copy in copies[4:]:
        copy.wait()
    total = fold(dot(jnp.concatenate(inner, 1), hidden[...], NN)) + acc[...]
    for k in range(32):
        out[k] = total[8 * (k % 4):8 * (k % 4) + 8, 128 * (k // 4):128 * (k // 4) + 128]


def left_partial(q_t, key, error, hidden):
    big = pltpu.VMEM((WIDTH, WIDTH), BF16)
    thin = pltpu.VMEM((RANK, WIDTH), F32)
    return pl.pallas_call(
        left_kernel,
        out_shape=(pltpu.VMEM((32, 8, 128), F32), big, big, big),
        in_specs=[HBM] * 4,
        out_specs=(VMEM,) * 4,
        scratch_shapes=[thin, thin, pltpu.SemaphoreType.DMA((7,))],
        compiler_params=PARAMS,
        name="left_partial",
    )(*in_hbm(q_t, key, error, hidden))


def left_sum_kernel(parts, out):
    total = jnp.sum(parts[...], 0)
    total = total + pltpu.roll(total, 4, 0)
    for k in range(32):
        out[k] = total


def left_sum(parts):
    return pl.pallas_call(
        left_sum_kernel,
        out_shape=pltpu.VMEM((32, 8, 128), F32),
        in_specs=[VMEM],
        out_specs=VMEM,
        compiler_params=PARAMS,
        name="left_sum",
    )(*in_vmem(parts))


def right_kernel(tiles, key, error, hidden, out, gram):
    columns = [
        jnp.concatenate([tiles[4 * b + a] for a in range(4)], 0) for b in range(8)
    ]
    p3 = pieces(jnp.concatenate(columns, 1) * (1 / 64))
    square = fold(dot(p3, p3, NT))
    gram[...] = square[:, :RANK] + square[:, RANK:2 * RANK] + square[:, 2 * RANK:]
    quarter = 2 * lax.axis_index("z0") + lax.axis_index("y0")
    own = gram[pl.ds(pl.multiple_of(8 * quarter, 8), 8), :]
    packed = jnp.concatenate([own[2 * i:2 * i + 2] for i in range(4)], 1)
    inner = pieces(fold(dot(p3, hidden[...], NT)))
    total = (fold(dot(p3, error[...], NN)) + fold(dot(inner, key[...], NN))) * (1 / 64)
    for m in range(8):
        for s in range(4):
            at = ROWS * (4 * m + s)
            out[at:at + 8, :] = total[8 * s:8 * s + 8, 128 * m:128 * m + 128]
            out[at + 8:at + ROWS, :] = packed


def right_partial(tiles, key, error, hidden):
    return pl.pallas_call(
        right_kernel,
        out_shape=pltpu.VMEM((32 * ROWS, 128), F32),
        in_specs=[VMEM] * 4,
        out_specs=VMEM,
        scratch_shapes=[pltpu.VMEM((RANK, RANK), F32)],
        compiler_params=PARAMS,
        name="right_partial",
    )(*in_vmem(tiles, key, error, hidden))


def right_sum_kernel(parts, out, gram):
    total = parts[:8, :]
    for k in range(1, 32):
        total = total + parts[ROWS * k:ROWS * k + 8, :]
    for k in range(64):
        out[k] = total
    for s in range(4):
        packed = parts[ROWS * s + 8:ROWS * s + ROWS, :]
        for m in range(1, 8):
            at = ROWS * (4 * m + s)
            packed = packed + parts[at + 8:at + ROWS, :]
        for i in range(4):
            gram[8 * s + 2 * i:8 * s + 2 * i + 2, :RANK] = packed[:, RANK * i:RANK * i + RANK]


def right_sum(parts):
    return pl.pallas_call(
        right_sum_kernel,
        out_shape=(pltpu.VMEM((64, 8, 128), F32), pltpu.VMEM((RANK, 128), F32)),
        in_specs=[VMEM],
        out_specs=(VMEM, VMEM),
        compiler_params=PARAMS,
        name="right_sum",
    )(*in_vmem(parts))


def along_lanes(tile, j):
    return jnp.broadcast_to(tile[:, j:j + 1], (8, 128))


def along_rows(tile, j):
    return jnp.broadcast_to(tile[j:j + 1, :], (8, 128))


def finish_kernel(tiles, gram, out):
    rows = [jnp.sum(tiles[16 * s:16 * s + 16], 0) for s in (0, 2, 1, 3)]
    rest = [gram[8 * s:8 * s + 8, :] for s in range(4)]
    row = lax.broadcasted_iota(jnp.int32, (8, 128), 0)
    for b in range(4):
        column = {s: [along_lanes(rest[s], 8 * b + q) for q in range(8)] for s in range(b, 4)}
        block = [[along_rows(column[b][q], p) for q in range(p + 1)] for p in range(8)]
        pivot_rest = [along_rows(rest[b], p) for p in range(8)]
        pivot_rows = [along_rows(rows[b], p) for p in range(8)]
        inverse = []
        for q in range(8):
            inverse.append(1.0 / block[q][q])
            for p in range(q + 1, 8):
                factor = block[p][q] * inverse[q]
                pivot_rest[p] = pivot_rest[p] - factor * pivot_rest[q]
                pivot_rows[p] = pivot_rows[p] - factor * pivot_rows[q]
                for t in range(q + 1, p + 1):
                    block[p][t] = block[p][t] - factor * block[t][q]
        for s in range(b, 4):
            for q in range(8):
                factor = column[s][q] * inverse[q]
                if s == b:
                    factor = jnp.where(row > q, factor, 0.0)
                for t in range(q + 1, 8):
                    column[s][t] = column[s][t] - factor * block[t][q]
                rest[s] = rest[s] - factor * pivot_rest[q]
                rows[s] = rows[s] - factor * pivot_rows[q]
        scale = lax.rsqrt(block[0][0])
        for q in range(1, 8):
            scale = jnp.where(row == q, lax.rsqrt(block[q][q]), scale)
        out[8 * b:8 * b + 8, :] = rows[b] * scale


def finish(tiles, gram):
    return pl.pallas_call(
        finish_kernel,
        out_shape=jax.ShapeDtypeStruct((RANK, 128), F32),
        in_specs=[VMEM, VMEM],
        out_specs=VMEM,
        compiler_params=PARAMS,
        name="finish",
    )(*in_vmem(tiles, gram))


def halves_over_dp(tiles):
    return lax.all_to_all(tiles.reshape(64, 4, 128), STEP_DP, 0, 0, tiled=True).reshape(32, 8, 128)


def shards(hidden, key, error, q_init):
    error = error[0]
    part, key, error, hidden = left_partial(q_init.T, key, error, hidden)
    tiles = halves_over_dp(left_sum(halves_over_dp(part)))
    part = right_partial(tiles, key, error, hidden).reshape(-1, 2, 128)
    part = lax.all_to_all(part, NEAR, 0, 0, tiled=True).reshape(-1, 128)
    tiles, gram = right_sum(part)
    return finish(lax.all_to_all(tiles, STEP_DP, 0, 0, tiled=True), gram).T


def solution(mesh):
    fine = Mesh(mesh.devices.reshape(2, 2, 2, 2, 2, 2, 4, 2), DP + MP)
    in_specs = (P(DP, MP), P(DP, None), P(DP, MP, None), P())
    return jax.shard_map(shards, mesh=fine, in_specs=in_specs, out_specs=P(MP, None), check_vma=False)
```

```python
import jax
import jax.experimental.pallas as pl
import jax.experimental.pallas.tpu as pltpu
import jax.numpy as jnp
from jax import lax
from jax.sharding import Mesh, PartitionSpec as P

DP = ("z2", "z1", "z0", "y2", "y1", "y0")
MP = ("x", "core")
STEP_DP = ("y0", "z0", "y1", "z1", "y2", "z2")
NEAR = ("x", "core", "z0", "y0")

F32, BF16 = jnp.float32, jnp.bfloat16
RANK, WIDTH, HALF = 32, 1024, 512
ROWS = 10
NN = (((1,), (0,)), ((), ()))
NT = (((1,), (1,)), ((), ()))
VMEM = pl.BlockSpec(memory_space=pltpu.VMEM)
HBM = pl.BlockSpec(memory_space=pltpu.HBM)
PARAMS = pltpu.CompilerParams(vmem_limit_bytes=24 << 20)


def in_vmem(*arrays):
    return [pltpu.with_memory_space_constraint(a, pltpu.VMEM) for a in arrays]


def in_hbm(*arrays):
    return [pltpu.with_memory_space_constraint(a, pltpu.HBM) for a in arrays]


def dot(a, b, dims):
    return lax.dot_general(a, b, dims, preferred_element_type=F32)


def pieces(value):
    parts = []
    for _ in range(3):
        parts.append(value.astype(BF16))
        value = value - parts[-1].astype(F32)
    return jnp.concatenate(parts, 0)


def fold(product):
    return product[:RANK] + product[RANK:2 * RANK] + product[2 * RANK:]


def left_kernel(q_hbm, key_hbm, error_hbm, hidden_hbm, out, key, error, hidden, q, acc, sems):
    first = pltpu.make_async_copy(q_hbm, q, sems.at[0])
    first.start()
    copies = []
    for source, target in ((key_hbm, key), (error_hbm, error), (hidden_hbm, hidden)):
        for at in range(0, WIDTH, HALF):
            rows = pl.ds(at, HALF)
            copies.append(pltpu.make_async_copy(source.at[rows, :], target.at[rows, :], sems.at[1 + len(copies)]))
            copies[-1].start()
    first.wait()
    q2 = pieces(q[...])
    inner = []
    for i in range(2):
        copies[i].wait()
        inner.append(pieces(fold(dot(q2, key[i * HALF:(i + 1) * HALF, :], NT))))
    for i in range(2):
        copies[2 + i].wait()
        acc[:, i * HALF:(i + 1) * HALF] = fold(dot(q2, error[i * HALF:(i + 1) * HALF, :], NT))
    for copy in copies[4:]:
        copy.wait()
    total = fold(dot(jnp.concatenate(inner, 1), hidden[...], NN)) + acc[...]
    for k in range(32):
        out[k] = total[8 * (k % 4):8 * (k % 4) + 8, 128 * (k // 4):128 * (k // 4) + 128]


def left_partial(q_t, key, error, hidden):
    big = pltpu.VMEM((WIDTH, WIDTH), BF16)
    thin = pltpu.VMEM((RANK, WIDTH), F32)
    return pl.pallas_call(
        left_kernel,
        out_shape=(pltpu.VMEM((32, 8, 128), F32), big, big, big),
        in_specs=[HBM] * 4,
        out_specs=(VMEM,) * 4,
        scratch_shapes=[thin, thin, pltpu.SemaphoreType.DMA((7,))],
        compiler_params=PARAMS,
        name="left_partial",
    )(*in_hbm(q_t, key, error, hidden))


def left_sum_kernel(parts, out):
    total = jnp.sum(parts[...], 0)
    total = total + pltpu.roll(total, 4, 0)
    for k in range(32):
        out[k] = total


def left_sum(parts):
    return pl.pallas_call(
        left_sum_kernel,
        out_shape=pltpu.VMEM((32, 8, 128), F32),
        in_specs=[VMEM],
        out_specs=VMEM,
        compiler_params=PARAMS,
        name="left_sum",
    )(*in_vmem(parts))


def right_kernel(tiles, key, error, hidden, out, gram):
    columns = [
        jnp.concatenate([tiles[4 * b + a] for a in range(4)], 0) for b in range(8)
    ]
    p3 = pieces(jnp.concatenate(columns, 1) * (1 / 64))
    square = fold(dot(p3, p3, NT))
    gram[...] = square[:, :RANK] + square[:, RANK:2 * RANK] + square[:, 2 * RANK:]
    quarter = 2 * lax.axis_index("z0") + lax.axis_index("y0")
    own = gram[pl.ds(pl.multiple_of(8 * quarter, 8), 8), :]
    packed = jnp.concatenate([own[2 * i:2 * i + 2] for i in range(4)], 1)
    inner = pieces(fold(dot(p3, hidden[...], NT)))
    total = (fold(dot(p3, error[...], NN)) + fold(dot(inner, key[...], NN))) * (1 / 64)
    for m in range(8):
        for s in range(4):
            at = ROWS * (4 * m + s)
            out[at:at + 8, :] = total[8 * s:8 * s + 8, 128 * m:128 * m + 128]
            out[at + 8:at + ROWS, :] = packed


def right_partial(tiles, key, error, hidden):
    return pl.pallas_call(
        right_kernel,
        out_shape=pltpu.VMEM((32 * ROWS, 128), F32),
        in_specs=[VMEM] * 4,
        out_specs=VMEM,
        scratch_shapes=[pltpu.VMEM((RANK, RANK), F32)],
        compiler_params=PARAMS,
        name="right_partial",
    )(*in_vmem(tiles, key, error, hidden))


def along_lanes(tile, j):
    return jnp.broadcast_to(tile[:, j:j + 1], (8, 128))


def along_rows(tile, j):
    return jnp.broadcast_to(tile[j:j + 1, :], (8, 128))


def eliminate(gram, rows, out):
    rows = list(rows)
    rest = [gram[8 * s:8 * s + 8, :] for s in range(4)]
    row = lax.broadcasted_iota(jnp.int32, (8, 128), 0)
    for b in range(4):
        column = {s: [along_lanes(rest[s], 8 * b + q) for q in range(8)] for s in range(b, 4)}
        block = [[along_rows(column[b][q], p) for q in range(p + 1)] for p in range(8)]
        pivot_rest = [along_rows(rest[b], p) for p in range(8)]
        pivot_rows = [along_rows(rows[b], p) for p in range(8)]
        inverse = []
        for q in range(8):
            inverse.append(1.0 / block[q][q])
            for p in range(q + 1, 8):
                factor = block[p][q] * inverse[q]
                pivot_rest[p] = pivot_rest[p] - factor * pivot_rest[q]
                pivot_rows[p] = pivot_rows[p] - factor * pivot_rows[q]
                for t in range(q + 1, p + 1):
                    block[p][t] = block[p][t] - factor * block[t][q]
        for s in range(b, 4):
            for q in range(8):
                factor = column[s][q] * inverse[q]
                if s == b:
                    factor = jnp.where(row > q, factor, 0.0)
                for t in range(q + 1, 8):
                    column[s][t] = column[s][t] - factor * block[t][q]
                rest[s] = rest[s] - factor * pivot_rest[q]
                rows[s] = rows[s] - factor * pivot_rows[q]
        scale = lax.rsqrt(block[0][0])
        for q in range(1, 8):
            scale = jnp.where(row == q, lax.rsqrt(block[q][q]), scale)
        out[8 * b:8 * b + 8, :] = rows[b] * scale


def right_sum_kernel(parts, out, factor):
    total = parts[:8, :]
    for k in range(1, 32):
        total = total + parts[ROWS * k:ROWS * k + 8, :]
    for k in range(64):
        out[k] = total
    for s in range(4):
        packed = parts[ROWS * s + 8:ROWS * s + ROWS, :]
        for m in range(1, 8):
            at = ROWS * (4 * m + s)
            packed = packed + parts[at + 8:at + ROWS, :]
        for i in range(4):
            factor[8 * s + 2 * i:8 * s + 2 * i + 2, :RANK] = packed[:, RANK * i:RANK * i + RANK]

    @pl.when(lax.axis_index("core") == 0)
    def _():
        lane = lax.broadcasted_iota(jnp.int32, (8, 128), 1)
        row = lax.broadcasted_iota(jnp.int32, (8, 128), 0)
        eliminate(factor, [jnp.where(lane == row + 8 * s, 1.0, 0.0) for s in range(4)], factor)


def right_sum(parts):
    return pl.pallas_call(
        right_sum_kernel,
        out_shape=(pltpu.VMEM((64, 8, 128), F32), pltpu.VMEM((RANK, 128), F32)),
        in_specs=[VMEM],
        out_specs=(VMEM, VMEM),
        compiler_params=PARAMS,
        name="right_sum",
    )(*in_vmem(parts))


def finish_kernel(tiles, factor, out):
    rows = [jnp.sum(tiles[16 * s:16 * s + 16], 0) for s in (0, 2, 1, 3)]

    @pl.when(lax.axis_index("core") == 0)
    def _():
        out[...] = jnp.dot(
            factor[:, :RANK], jnp.concatenate(rows, 0), precision=lax.Precision.HIGHEST, preferred_element_type=F32
        )

    @pl.when(lax.axis_index("core") != 0)
    def _():
        eliminate(factor, rows, out)


def finish(tiles, factor):
    return pl.pallas_call(
        finish_kernel,
        out_shape=jax.ShapeDtypeStruct((RANK, 128), F32),
        in_specs=[VMEM, VMEM],
        out_specs=VMEM,
        compiler_params=PARAMS,
        name="finish",
    )(*in_vmem(tiles, factor))


def halves_over_dp(tiles):
    return lax.all_to_all(tiles.reshape(64, 4, 128), STEP_DP, 0, 0, tiled=True).reshape(32, 8, 128)


def shards(hidden, key, error, q_init):
    error = error[0]
    part, key, error, hidden = left_partial(q_init.T, key, error, hidden)
    tiles = halves_over_dp(left_sum(halves_over_dp(part)))
    part = right_partial(tiles, key, error, hidden).reshape(-1, 2, 128)
    part = lax.all_to_all(part, NEAR, 0, 0, tiled=True).reshape(-1, 128)
    tiles, factor = right_sum(part)
    return finish(lax.all_to_all(tiles, STEP_DP, 0, 0, tiled=True), factor).T


def solution(mesh):
    fine = Mesh(mesh.devices.reshape(2, 2, 2, 2, 2, 2, 4, 2), DP + MP)
    in_specs = (P(DP, MP), P(DP, None), P(DP, MP, None), P())
    return jax.shard_map(shards, mesh=fine, in_specs=in_specs, out_specs=P(MP, None), check_vma=False)
```

```python
import jax
import jax.experimental.pallas as pl
import jax.experimental.pallas.tpu as pltpu
import jax.numpy as jnp
from jax import lax
from jax.sharding import Mesh, PartitionSpec as P

DP = ("z2", "z1", "z0", "y2", "y1", "y0")
MP = ("x", "core")
STEP_DP = ("y0", "z0", "y1", "z1", "z2", "y2")
NEAR = ("x", "core", "z0", "y0")

F32, BF16 = jnp.float32, jnp.bfloat16
RANK, WIDTH, HALF = 32, 1024, 512
ROWS = 10
NN = (((1,), (0,)), ((), ()))
NT = (((1,), (1,)), ((), ()))
VMEM = pl.BlockSpec(memory_space=pltpu.VMEM)
HBM = pl.BlockSpec(memory_space=pltpu.HBM)
PARAMS = pltpu.CompilerParams(vmem_limit_bytes=24 << 20)


def in_vmem(*arrays):
    return [pltpu.with_memory_space_constraint(a, pltpu.VMEM) for a in arrays]


def in_hbm(*arrays):
    return [pltpu.with_memory_space_constraint(a, pltpu.HBM) for a in arrays]


def dot(a, b, dims):
    return lax.dot_general(a, b, dims, preferred_element_type=F32)


def pieces(value):
    parts = []
    for _ in range(3):
        parts.append(value.astype(BF16))
        value = value - parts[-1].astype(F32)
    return jnp.concatenate(parts, 0)


def fold(product):
    return product[:RANK] + product[RANK:2 * RANK] + product[2 * RANK:]


def left_kernel(q_hbm, key_hbm, error_hbm, hidden_hbm, out, key, error, hidden, q, acc, sems):
    first = pltpu.make_async_copy(q_hbm, q, sems.at[0])
    first.start()
    copies = []
    for source, target in ((key_hbm, key), (error_hbm, error), (hidden_hbm, hidden)):
        for at in range(0, WIDTH, HALF):
            rows = pl.ds(at, HALF)
            copies.append(pltpu.make_async_copy(source.at[rows, :], target.at[rows, :], sems.at[1 + len(copies)]))
            copies[-1].start()
    first.wait()
    q2 = pieces(q[...])
    inner = []
    for i in range(2):
        copies[i].wait()
        inner.append(pieces(fold(dot(q2, key[i * HALF:(i + 1) * HALF, :], NT))))
    for i in range(2):
        copies[2 + i].wait()
        acc[:, i * HALF:(i + 1) * HALF] = fold(dot(q2, error[i * HALF:(i + 1) * HALF, :], NT))
    for copy in copies[4:]:
        copy.wait()
    total = fold(dot(jnp.concatenate(inner, 1), hidden[...], NN)) + acc[...]
    for k in range(32):
        out[k] = total[8 * (k % 4):8 * (k % 4) + 8, 128 * (k // 4):128 * (k // 4) + 128]


def left_partial(q_t, key, error, hidden):
    big = pltpu.VMEM((WIDTH, WIDTH), BF16)
    thin = pltpu.VMEM((RANK, WIDTH), F32)
    return pl.pallas_call(
        left_kernel,
        out_shape=(pltpu.VMEM((32, 8, 128), F32), big, big, big),
        in_specs=[HBM] * 4,
        out_specs=(VMEM,) * 4,
        scratch_shapes=[thin, thin, pltpu.SemaphoreType.DMA((7,))],
        compiler_params=PARAMS,
        name="left_partial",
    )(*in_hbm(q_t, key, error, hidden))


def left_sum_kernel(parts, out):
    total = jnp.sum(parts[...], 0)
    total = total + pltpu.roll(total, 4, 0)
    for k in range(32):
        out[k] = total


def left_sum(parts):
    return pl.pallas_call(
        left_sum_kernel,
        out_shape=pltpu.VMEM((32, 8, 128), F32),
        in_specs=[VMEM],
        out_specs=VMEM,
        compiler_params=PARAMS,
        name="left_sum",
    )(*in_vmem(parts))


def right_kernel(tiles, key, error, hidden, out, gram):
    columns = [
        jnp.concatenate([tiles[4 * b + a] for a in range(4)], 0) for b in range(8)
    ]
    p3 = pieces(jnp.concatenate(columns, 1) * (1 / 64))
    square = fold(dot(p3, p3, NT))
    gram[...] = square[:, :RANK] + square[:, RANK:2 * RANK] + square[:, 2 * RANK:]
    quarter = 2 * lax.axis_index("z0") + lax.axis_index("y0")
    own = gram[pl.ds(pl.multiple_of(8 * quarter, 8), 8), :]
    packed = jnp.concatenate([own[2 * i:2 * i + 2] for i in range(4)], 1)
    inner = pieces(fold(dot(p3, hidden[...], NT)))
    total = (fold(dot(p3, error[...], NN)) + fold(dot(inner, key[...], NN))) * (1 / 64)
    for m in range(8):
        for s in range(4):
            at = ROWS * (4 * m + s)
            out[at:at + 8, :] = total[8 * s:8 * s + 8, 128 * m:128 * m + 128]
            out[at + 8:at + ROWS, :] = packed


def right_partial(tiles, key, error, hidden):
    return pl.pallas_call(
        right_kernel,
        out_shape=pltpu.VMEM((32 * ROWS, 128), F32),
        in_specs=[VMEM] * 4,
        out_specs=VMEM,
        scratch_shapes=[pltpu.VMEM((RANK, RANK), F32)],
        compiler_params=PARAMS,
        name="right_partial",
    )(*in_vmem(tiles, key, error, hidden))


def along_lanes(tile, j):
    return jnp.broadcast_to(tile[:, j:j + 1], (8, 128))


def along_rows(tile, j):
    return jnp.broadcast_to(tile[j:j + 1, :], (8, 128))


def eliminate(gram, rows, out):
    rows = list(rows)
    rest = [gram[8 * s:8 * s + 8, :] for s in range(4)]
    row = lax.broadcasted_iota(jnp.int32, (8, 128), 0)
    for b in range(4):
        column = {s: [along_lanes(rest[s], 8 * b + q) for q in range(8)] for s in range(b, 4)}
        block = [[along_rows(column[b][q], p) for q in range(p + 1)] for p in range(8)]
        pivot_rest = [along_rows(rest[b], p) for p in range(8)]
        pivot_rows = [along_rows(rows[b], p) for p in range(8)]
        inverse = []
        for q in range(8):
            inverse.append(1.0 / block[q][q])
            for p in range(q + 1, 8):
                factor = block[p][q] * inverse[q]
                pivot_rest[p] = pivot_rest[p] - factor * pivot_rest[q]
                pivot_rows[p] = pivot_rows[p] - factor * pivot_rows[q]
                for t in range(q + 1, p + 1):
                    block[p][t] = block[p][t] - factor * block[t][q]
        for s in range(b, 4):
            for q in range(8):
                factor = column[s][q] * inverse[q]
                if s == b:
                    factor = jnp.where(row > q, factor, 0.0)
                for t in range(q + 1, 8):
                    column[s][t] = column[s][t] - factor * block[t][q]
                rest[s] = rest[s] - factor * pivot_rest[q]
                rows[s] = rows[s] - factor * pivot_rows[q]
        scale = lax.rsqrt(block[0][0])
        for q in range(1, 8):
            scale = jnp.where(row == q, lax.rsqrt(block[q][q]), scale)
        out[8 * b:8 * b + 8, :] = rows[b] * scale


def right_sum_kernel(parts, out, factor):
    total = parts[:8, :]
    for k in range(1, 32):
        total = total + parts[ROWS * k:ROWS * k + 8, :]
    for k in range(64):
        out[k] = total
    for s in range(4):
        packed = parts[ROWS * s + 8:ROWS * s + ROWS, :]
        for m in range(1, 8):
            at = ROWS * (4 * m + s)
            packed = packed + parts[at + 8:at + ROWS, :]
        for i in range(4):
            factor[8 * s + 2 * i:8 * s + 2 * i + 2, :RANK] = packed[:, RANK * i:RANK * i + RANK]

    @pl.when(lax.axis_index("core") == 0)
    def _():
        lane = lax.broadcasted_iota(jnp.int32, (8, 128), 1)
        row = lax.broadcasted_iota(jnp.int32, (8, 128), 0)
        eliminate(factor, [jnp.where(lane == row + 8 * s, 1.0, 0.0) for s in range(4)], factor)


def right_sum(parts):
    return pl.pallas_call(
        right_sum_kernel,
        out_shape=(pltpu.VMEM((64, 8, 128), F32), pltpu.VMEM((RANK, 128), F32)),
        in_specs=[VMEM],
        out_specs=(VMEM, VMEM),
        compiler_params=PARAMS,
        name="right_sum",
    )(*in_vmem(parts))


def finish_kernel(tiles, factor, out):
    rows = [jnp.sum(tiles[16 * s:16 * s + 16], 0) for s in (0, 2, 1, 3)]

    @pl.when(lax.axis_index("core") == 0)
    def _():
        out[...] = jnp.dot(
            factor[:, :RANK], jnp.concatenate(rows, 0), precision=lax.Precision.HIGHEST, preferred_element_type=F32
        )

    @pl.when(lax.axis_index("core") != 0)
    def _():
        eliminate(factor, rows, out)


def finish(tiles, factor):
    return pl.pallas_call(
        finish_kernel,
        out_shape=jax.ShapeDtypeStruct((RANK, 128), F32),
        in_specs=[VMEM, VMEM],
        out_specs=VMEM,
        compiler_params=PARAMS,
        name="finish",
    )(*in_vmem(tiles, factor))


def halves_over_dp(tiles):
    return lax.all_to_all(tiles.reshape(64, 4, 128), STEP_DP, 0, 0, tiled=True).reshape(32, 8, 128)


def shards(hidden, key, error, q_init):
    error = error[0]
    part, key, error, hidden = left_partial(q_init.T, key, error, hidden)
    tiles = halves_over_dp(left_sum(halves_over_dp(part)))
    part = right_partial(tiles, key, error, hidden).reshape(-1, 2, 128)
    part = lax.all_to_all(part, NEAR, 0, 0, tiled=True).reshape(-1, 128)
    tiles, factor = right_sum(part)
    return finish(lax.all_to_all(tiles, STEP_DP, 0, 0, tiled=True), factor).T


def solution(mesh):
    fine = Mesh(mesh.devices.reshape(2, 2, 2, 2, 2, 2, 4, 2), DP + MP)
    in_specs = (P(DP, MP), P(DP, None), P(DP, MP, None), P())
    return jax.shard_map(shards, mesh=fine, in_specs=in_specs, out_specs=P(MP, None), check_vma=False)
```

```python
import jax
import jax.experimental.pallas as pl
import jax.experimental.pallas.tpu as pltpu
import jax.numpy as jnp
from jax import lax
from jax.sharding import Mesh, PartitionSpec as P

DP = ("z2", "z1", "z0", "y2", "y1", "y0")
MP = ("x", "core")
STEP_DP = ("y0", "z0", "y1", "z1", "y2", "z2")
NEAR = ("x", "core", "z0", "y0")

F32, BF16 = jnp.float32, jnp.bfloat16
RANK, WIDTH, HALF = 32, 1024, 512
ROWS = 10
NN = (((1,), (0,)), ((), ()))
NT = (((1,), (1,)), ((), ()))
VMEM = pl.BlockSpec(memory_space=pltpu.VMEM)
HBM = pl.BlockSpec(memory_space=pltpu.HBM)
PARAMS = pltpu.CompilerParams(vmem_limit_bytes=24 << 20)


def in_vmem(*arrays):
    return [pltpu.with_memory_space_constraint(a, pltpu.VMEM) for a in arrays]


def in_hbm(*arrays):
    return [pltpu.with_memory_space_constraint(a, pltpu.HBM) for a in arrays]


def dot(a, b, dims):
    return lax.dot_general(a, b, dims, preferred_element_type=F32)


def pieces(value):
    parts = []
    for _ in range(3):
        parts.append(value.astype(BF16))
        value = value - parts[-1].astype(F32)
    return jnp.concatenate(parts, 0)


def fold(product):
    return product[:RANK] + product[RANK:2 * RANK] + product[2 * RANK:]


def left_kernel(q_hbm, key_hbm, error_hbm, hidden_hbm, out, key, error, hidden, q, acc, sems):
    first = pltpu.make_async_copy(q_hbm, q, sems.at[0])
    first.start()
    copies = []
    for source, target in ((key_hbm, key), (error_hbm, error), (hidden_hbm, hidden)):
        for at in range(0, WIDTH, HALF):
            rows = pl.ds(at, HALF)
            copies.append(pltpu.make_async_copy(source.at[rows, :], target.at[rows, :], sems.at[1 + len(copies)]))
            copies[-1].start()
    first.wait()
    q2 = pieces(q[...])
    inner = []
    for i in range(2):
        copies[i].wait()
        inner.append(pieces(fold(dot(q2, key[i * HALF:(i + 1) * HALF, :], NT))))
    for i in range(2):
        copies[2 + i].wait()
        acc[:, i * HALF:(i + 1) * HALF] = fold(dot(q2, error[i * HALF:(i + 1) * HALF, :], NT))
    for copy in copies[4:]:
        copy.wait()
    total = fold(dot(jnp.concatenate(inner, 1), hidden[...], NN)) + acc[...]
    for k in range(32):
        out[k] = total[8 * (k % 4):8 * (k % 4) + 8, 128 * (k // 4):128 * (k // 4) + 128]

    @pl.when(lax.axis_index("core") == 0)
    def _():
        hidden[...] = jnp.transpose(hidden[...])


def left_partial(q_t, key, error, hidden):
    big = pltpu.VMEM((WIDTH, WIDTH), BF16)
    thin = pltpu.VMEM((RANK, WIDTH), F32)
    return pl.pallas_call(
        left_kernel,
        out_shape=(pltpu.VMEM((32, 8, 128), F32), big, big, big),
        in_specs=[HBM] * 4,
        out_specs=(VMEM,) * 4,
        scratch_shapes=[thin, thin, pltpu.SemaphoreType.DMA((7,))],
        compiler_params=PARAMS,
        name="left_partial",
    )(*in_hbm(q_t, key, error, hidden))


def left_sum_kernel(parts, out):
    total = jnp.sum(parts[...], 0)
    total = total + pltpu.roll(total, 4, 0)
    for k in range(32):
        out[k] = total


def left_sum(parts):
    return pl.pallas_call(
        left_sum_kernel,
        out_shape=pltpu.VMEM((32, 8, 128), F32),
        in_specs=[VMEM],
        out_specs=VMEM,
        compiler_params=PARAMS,
        name="left_sum",
    )(*in_vmem(parts))


def right_kernel(*refs):
    @pl.when(lax.axis_index("core") == 0)
    def _():
        right_factor(NN, *refs)

    @pl.when(lax.axis_index("core") != 0)
    def _():
        right_factor(NT, *refs)


def right_factor(dims, tiles, key, error, hidden, out, gram):
    columns = [
        jnp.concatenate([tiles[4 * b + a] for a in range(4)], 0) for b in range(8)
    ]
    p3 = pieces(jnp.concatenate(columns, 1) * (1 / 64))
    square = fold(dot(p3, p3, NT))
    gram[...] = square[:, :RANK] + square[:, RANK:2 * RANK] + square[:, 2 * RANK:]
    quarter = 2 * lax.axis_index("z0") + lax.axis_index("y0")
    own = gram[pl.ds(pl.multiple_of(8 * quarter, 8), 8), :]
    packed = jnp.concatenate([own[2 * i:2 * i + 2] for i in range(4)], 1)
    inner = pieces(fold(dot(p3, hidden[...], dims)))
    total = (fold(dot(p3, error[...], NN)) + fold(dot(inner, key[...], NN))) * (1 / 64)
    for m in range(8):
        for s in range(4):
            at = ROWS * (4 * m + s)
            out[at:at + 8, :] = total[8 * s:8 * s + 8, 128 * m:128 * m + 128]
            out[at + 8:at + ROWS, :] = packed


def right_partial(tiles, key, error, hidden):
    return pl.pallas_call(
        right_kernel,
        out_shape=pltpu.VMEM((32 * ROWS, 128), F32),
        in_specs=[VMEM] * 4,
        out_specs=VMEM,
        scratch_shapes=[pltpu.VMEM((RANK, RANK), F32)],
        compiler_params=PARAMS,
        name="right_partial",
    )(*in_vmem(tiles, key, error, hidden))


def along_lanes(tile, j):
    return jnp.broadcast_to(tile[:, j:j + 1], (8, 128))


def along_rows(tile, j):
    return jnp.broadcast_to(tile[j:j + 1, :], (8, 128))


def eliminate(gram, rows, out):
    rows = list(rows)
    rest = [gram[8 * s:8 * s + 8, :] for s in range(4)]
    row = lax.broadcasted_iota(jnp.int32, (8, 128), 0)
    for b in range(4):
        column = {s: [along_lanes(rest[s], 8 * b + q) for q in range(8)] for s in range(b, 4)}
        block = [[along_rows(column[b][q], p) for q in range(p + 1)] for p in range(8)]
        pivot_rest = [along_rows(rest[b], p) for p in range(8)]
        pivot_rows = [along_rows(rows[b], p) for p in range(8)]
        inverse = []
        for q in range(8):
            inverse.append(1.0 / block[q][q])
            for p in range(q + 1, 8):
                factor = block[p][q] * inverse[q]
                pivot_rest[p] = pivot_rest[p] - factor * pivot_rest[q]
                pivot_rows[p] = pivot_rows[p] - factor * pivot_rows[q]
                for t in range(q + 1, p + 1):
                    block[p][t] = block[p][t] - factor * block[t][q]
        for s in range(b, 4):
            for q in range(8):
                factor = column[s][q] * inverse[q]
                if s == b:
                    factor = jnp.where(row > q, factor, 0.0)
                for t in range(q + 1, 8):
                    column[s][t] = column[s][t] - factor * block[t][q]
                rest[s] = rest[s] - factor * pivot_rest[q]
                rows[s] = rows[s] - factor * pivot_rows[q]
        scale = lax.rsqrt(block[0][0])
        for q in range(1, 8):
            scale = jnp.where(row == q, lax.rsqrt(block[q][q]), scale)
        out[8 * b:8 * b + 8, :] = rows[b] * scale


def right_sum_kernel(parts, out, factor):
    total = parts[:8, :]
    for k in range(1, 32):
        total = total + parts[ROWS * k:ROWS * k + 8, :]
    for k in range(64):
        out[k] = total
    for s in range(4):
        packed = parts[ROWS * s + 8:ROWS * s + ROWS, :]
        for m in range(1, 8):
            at = ROWS * (4 * m + s)
            packed = packed + parts[at + 8:at + ROWS, :]
        for i in range(4):
            factor[8 * s + 2 * i:8 * s + 2 * i + 2, :RANK] = packed[:, RANK * i:RANK * i + RANK]

    @pl.when(lax.axis_index("core") == 0)
    def _():
        lane = lax.broadcasted_iota(jnp.int32, (8, 128), 1)
        row = lax.broadcasted_iota(jnp.int32, (8, 128), 0)
        eliminate(factor, [jnp.where(lane == row + 8 * s, 1.0, 0.0) for s in range(4)], factor)


def right_sum(parts):
    return pl.pallas_call(
        right_sum_kernel,
        out_shape=(pltpu.VMEM((64, 8, 128), F32), pltpu.VMEM((RANK, 128), F32)),
        in_specs=[VMEM],
        out_specs=(VMEM, VMEM),
        compiler_params=PARAMS,
        name="right_sum",
    )(*in_vmem(parts))


def finish_kernel(tiles, factor, out):
    rows = [jnp.sum(tiles[16 * s:16 * s + 16], 0) for s in (0, 2, 1, 3)]

    @pl.when(lax.axis_index("core") == 0)
    def _():
        out[...] = jnp.dot(
            factor[:, :RANK], jnp.concatenate(rows, 0), precision=lax.Precision.HIGHEST, preferred_element_type=F32
        )

    @pl.when(lax.axis_index("core") != 0)
    def _():
        eliminate(factor, rows, out)


def finish(tiles, factor):
    return pl.pallas_call(
        finish_kernel,
        out_shape=jax.ShapeDtypeStruct((RANK, 128), F32),
        in_specs=[VMEM, VMEM],
        out_specs=VMEM,
        compiler_params=PARAMS,
        name="finish",
    )(*in_vmem(tiles, factor))


def halves_over_dp(tiles):
    return lax.all_to_all(tiles.reshape(64, 4, 128), STEP_DP, 0, 0, tiled=True).reshape(32, 8, 128)


def shards(hidden, key, error, q_init):
    error = error[0]
    part, key, error, hidden = left_partial(q_init.T, key, error, hidden)
    tiles = halves_over_dp(left_sum(halves_over_dp(part)))
    part = right_partial(tiles, key, error, hidden).reshape(-1, 2, 128)
    part = lax.all_to_all(part, NEAR, 0, 0, tiled=True).reshape(-1, 128)
    tiles, factor = right_sum(part)
    return finish(lax.all_to_all(tiles, STEP_DP, 0, 0, tiled=True), factor).T


def solution(mesh):
    fine = Mesh(mesh.devices.reshape(2, 2, 2, 2, 2, 2, 4, 2), DP + MP)
    in_specs = (P(DP, MP), P(DP, None), P(DP, MP, None), P())
    return jax.shard_map(shards, mesh=fine, in_specs=in_specs, out_specs=P(MP, None), check_vma=False)
```

```python
import jax
import jax.experimental.pallas as pl
import jax.experimental.pallas.tpu as pltpu
import jax.numpy as jnp
from jax import lax
from jax.sharding import Mesh, PartitionSpec as P

DP = ("z2", "z1", "z0", "y2", "y1", "y0")
MP = ("x", "core")
STEP_DP = ("y0", "z0", "y1", "z1", "y2", "z2")
NEAR = ("x", "core", "z0", "y0")

F32, BF16 = jnp.float32, jnp.bfloat16
RANK, WIDTH, HALF = 32, 1024, 512
ROWS = 10
NN = (((1,), (0,)), ((), ()))
NT = (((1,), (1,)), ((), ()))
VMEM = pl.BlockSpec(memory_space=pltpu.VMEM)
HBM = pl.BlockSpec(memory_space=pltpu.HBM)
PARAMS = pltpu.CompilerParams(vmem_limit_bytes=24 << 20)


def in_vmem(*arrays):
    return [pltpu.with_memory_space_constraint(a, pltpu.VMEM) for a in arrays]


def in_hbm(*arrays):
    return [pltpu.with_memory_space_constraint(a, pltpu.HBM) for a in arrays]


def dot(a, b, dims):
    return lax.dot_general(a, b, dims, preferred_element_type=F32)


def pieces(value):
    parts = []
    for _ in range(3):
        parts.append(value.astype(BF16))
        value = value - parts[-1].astype(F32)
    return jnp.concatenate(parts, 0)


def fold(product):
    return product[:RANK] + product[RANK:2 * RANK] + product[2 * RANK:]


def left_kernel(q_hbm, key_hbm, error_hbm, hidden_hbm, out, key, error, hidden, q, acc, sems):
    first = pltpu.make_async_copy(q_hbm, q, sems.at[0])
    first.start()
    copies = []
    for source, target in ((key_hbm, key), (error_hbm, error), (hidden_hbm, hidden)):
        for at in range(0, WIDTH, HALF):
            rows = pl.ds(at, HALF)
            copies.append(pltpu.make_async_copy(source.at[rows, :], target.at[rows, :], sems.at[1 + len(copies)]))
            copies[-1].start()
    first.wait()
    q2 = pieces(q[...])
    inner = []
    for i in range(2):
        copies[i].wait()
        inner.append(pieces(fold(dot(q2, key[i * HALF:(i + 1) * HALF, :], NT))))
    for i in range(2):
        copies[2 + i].wait()
        acc[:, i * HALF:(i + 1) * HALF] = fold(dot(q2, error[i * HALF:(i + 1) * HALF, :], NT))
    for copy in copies[4:]:
        copy.wait()
    total = fold(dot(jnp.concatenate(inner, 1), hidden[...], NN)) + acc[...]
    for k in range(32):
        out[k] = total[8 * (k % 4):8 * (k % 4) + 8, 128 * (k // 4):128 * (k // 4) + 128]


def left_partial(q_t, key, error, hidden):
    big = pltpu.VMEM((WIDTH, WIDTH), BF16)
    thin = pltpu.VMEM((RANK, WIDTH), F32)
    return pl.pallas_call(
        left_kernel,
        out_shape=(pltpu.VMEM((32, 8, 128), F32), big, big, big),
        in_specs=[HBM] * 4,
        out_specs=(VMEM,) * 4,
        scratch_shapes=[thin, thin, pltpu.SemaphoreType.DMA((7,))],
        compiler_params=PARAMS,
        name="left_partial",
    )(*in_hbm(q_t, key, error, hidden))


def left_sum_kernel(parts, out):
    total = jnp.sum(parts[...], 0)
    total = total + pltpu.roll(total, 4, 0)
    for k in range(32):
        out[k] = total


def left_sum(parts):
    return pl.pallas_call(
        left_sum_kernel,
        out_shape=pltpu.VMEM((32, 8, 128), F32),
        in_specs=[VMEM],
        out_specs=VMEM,
        compiler_params=PARAMS,
        name="left_sum",
    )(*in_vmem(parts))


def right_kernel(tiles, key, error, hidden, out, gram):
    columns = [
        jnp.concatenate([tiles[4 * b + a] for a in range(4)], 0) for b in range(8)
    ]
    p3 = pieces(jnp.concatenate(columns, 1) * (1 / 64))
    square = fold(dot(p3, p3, NT))
    gram[...] = square[:, :RANK] + square[:, RANK:2 * RANK] + square[:, 2 * RANK:]
    quarter = 2 * lax.axis_index("z0") + lax.axis_index("y0")
    own = gram[pl.ds(pl.multiple_of(8 * quarter, 8), 8), :]
    packed = jnp.concatenate([own[2 * i:2 * i + 2] for i in range(4)], 1)
    inner = pieces(fold(dot(p3, hidden[...], NT)))
    total = (fold(dot(p3, error[...], NN)) + fold(dot(inner, key[...], NN))) * (1 / 64)
    for m in range(8):
        for s in range(4):
            at = ROWS * (4 * m + s)
            out[at:at + 8, :] = total[8 * s:8 * s + 8, 128 * m:128 * m + 128]
            out[at + 8:at + ROWS, :] = packed


def right_partial(tiles, key, error, hidden):
    return pl.pallas_call(
        right_kernel,
        out_shape=pltpu.VMEM((32 * ROWS, 128), F32),
        in_specs=[VMEM] * 4,
        out_specs=VMEM,
        scratch_shapes=[pltpu.VMEM((RANK, RANK), F32)],
        compiler_params=PARAMS,
        name="right_partial",
    )(*in_vmem(tiles, key, error, hidden))


def along_lanes(tile, j):
    return jnp.broadcast_to(tile[:, j:j + 1], (8, 128))


def along_rows(tile, j):
    return jnp.broadcast_to(tile[j:j + 1, :], (8, 128))


def eliminate(gram, rows, out):
    rows = list(rows)
    rest = [gram[8 * s:8 * s + 8, :] for s in range(4)]
    row = lax.broadcasted_iota(jnp.int32, (8, 128), 0)
    for b in range(4):
        column = {s: [along_lanes(rest[s], 8 * b + q) for q in range(8)] for s in range(b, 4)}
        block = [[along_rows(column[b][q], p) for q in range(p + 1)] for p in range(8)]
        pivot_rest = [along_rows(rest[b], p) for p in range(8)]
        pivot_rows = [along_rows(rows[b], p) for p in range(8)]
        inverse = []
        for q in range(8):
            inverse.append(1.0 / block[q][q])
            for p in range(q + 1, 8):
                factor = block[p][q] * inverse[q]
                pivot_rest[p] = pivot_rest[p] - factor * pivot_rest[q]
                pivot_rows[p] = pivot_rows[p] - factor * pivot_rows[q]
                for t in range(q + 1, p + 1):
                    block[p][t] = block[p][t] - factor * block[t][q]
        for s in range(b, 4):
            for q in range(8):
                factor = column[s][q] * inverse[q]
                if s == b:
                    factor = jnp.where(row > q, factor, 0.0)
                for t in range(q + 1, 8):
                    column[s][t] = column[s][t] - factor * block[t][q]
                rest[s] = rest[s] - factor * pivot_rest[q]
                rows[s] = rows[s] - factor * pivot_rows[q]
        scale = lax.rsqrt(block[0][0])
        for q in range(1, 8):
            scale = jnp.where(row == q, lax.rsqrt(block[q][q]), scale)
        out[8 * b:8 * b + 8, :] = rows[b] * scale


def collect_gram(parts, gram):
    for s in range(4):
        packed = parts[ROWS * s + 8:ROWS * s + ROWS, :]
        for m in range(1, 8):
            at = ROWS * (4 * m + s)
            packed = packed + parts[at + 8:at + ROWS, :]
        for i in range(4):
            gram[8 * s + 2 * i:8 * s + 2 * i + 2, :RANK] = packed[:, RANK * i:RANK * i + RANK]


def right_sum_kernel(parts, out, factor):
    total = parts[:8, :]
    for k in range(1, 32):
        total = total + parts[ROWS * k:ROWS * k + 8, :]
    for k in range(64):
        out[k] = total

    @pl.when(lax.axis_index("core") == 0)
    def _():
        lane = lax.broadcasted_iota(jnp.int32, (8, 128), 1)
        row = lax.broadcasted_iota(jnp.int32, (8, 128), 0)
        collect_gram(parts, factor)
        eliminate(factor, [jnp.where(lane == row + 8 * s, 1.0, 0.0) for s in range(4)], factor)


def right_sum(parts):
    return pl.pallas_call(
        right_sum_kernel,
        out_shape=(pltpu.VMEM((64, 8, 128), F32), pltpu.VMEM((RANK, 128), F32)),
        in_specs=[VMEM],
        out_specs=(VMEM, VMEM),
        compiler_params=PARAMS,
        name="right_sum",
    )(*in_vmem(parts))


def finish_kernel(tiles, factor, parts, out, gram):
    rows = [jnp.sum(tiles[16 * s:16 * s + 16], 0) for s in (0, 2, 1, 3)]

    @pl.when(lax.axis_index("core") == 0)
    def _():
        out[...] = jnp.dot(
            factor[:, :RANK], jnp.concatenate(rows, 0), precision=lax.Precision.HIGHEST, preferred_element_type=F32
        )

    @pl.when(lax.axis_index("core") != 0)
    def _():
        collect_gram(parts, gram)
        eliminate(gram, rows, out)


def finish(tiles, factor, parts):
    return pl.pallas_call(
        finish_kernel,
        out_shape=jax.ShapeDtypeStruct((RANK, 128), F32),
        in_specs=[VMEM] * 3,
        out_specs=VMEM,
        scratch_shapes=[pltpu.VMEM((RANK, 128), F32)],
        compiler_params=PARAMS,
        name="finish",
    )(*in_vmem(tiles, factor, parts))


def halves_over_dp(tiles):
    return lax.all_to_all(tiles.reshape(64, 4, 128), STEP_DP, 0, 0, tiled=True).reshape(32, 8, 128)


def shards(hidden, key, error, q_init):
    error = error[0]
    part, key, error, hidden = left_partial(q_init.T, key, error, hidden)
    tiles = halves_over_dp(left_sum(halves_over_dp(part)))
    part = right_partial(tiles, key, error, hidden).reshape(-1, 2, 128)
    part = lax.all_to_all(part, NEAR, 0, 0, tiled=True).reshape(-1, 128)
    tiles, factor = right_sum(part)
    return finish(lax.all_to_all(tiles, STEP_DP, 0, 0, tiled=True), factor, part).T


def solution(mesh):
    fine = Mesh(mesh.devices.reshape(2, 2, 2, 2, 2, 2, 4, 2), DP + MP)
    in_specs = (P(DP, MP), P(DP, None), P(DP, MP, None), P())
    return jax.shard_map(shards, mesh=fine, in_specs=in_specs, out_specs=P(MP, None), check_vma=False)
```
